32 devices in a mesh: dp: 4 (over z), space: 8 (over y, x, core).
Axes of the slice: x: 2, y: 2, z: 4, core: 2. Of those that a mesh axis runs over, the one named last changes fastest.
Arguments:
- features: bfloat16 [4, 24, 64, 1024], P('dp', 'space'), may hold values from -6 to 6
- cotangent: bfloat16 [4, 24, 128, 128], P('dp', 'space'), may hold values from -6 to 6
- conv_one: bfloat16 [64, 1728], P('dp'), may hold values from -0.15625 to 0.15625
- down_weight: bfloat16 [128, 512], P('dp'), may hold values from -0.25 to 0.25
- conv_two: bfloat16 [128, 3456], P('dp'), may hold values from -0.109375 to 0.109375
- patch_home: int32 [16], replicated, may hold values from 0 to 23, as said below
- patch_links: int32 [16, 4], replicated, may hold values from -1 to 15, as said below
Outputs:
- level_two: bfloat16 [4, 24, 128, 128], P('dp', 'space')
- grad_conv_one: float32 [64, 1728], P('dp')
- grad_conv_down: float32 [128, 512], P('dp')
- grad_conv_two: float32 [128, 3456], P('dp')
The draws below stay inside these ranges and needn't reach their ends.
Inputs may be any that keep to these rules, and one draw needn't show every extreme that they name: Patch p sits on device patch_home[p] // 3 of the space axis in slot patch_home[p] % 3; no two patches share a slot; every device holds a run of consecutive patch numbers, the runs in the order of the devices, each of 1 to 3 patches; some device holds exactly 3 and some exactly one. `patch_links`: the patches form a grid of 2 columns and 8 rows, patch 2 r + c in row r and column c; the four entries of a patch name p - 1, p + 1, p - 2, p + 2 or -1 where the grid ends or the link is cut; links are symmetric; the first and the last row are linked across x.
All inputs are finite; a program needn't handle non-finite values.
Results may differ from the reference program's by a relative error of at most 0.014.
Values may be sent and summed in bfloat16 or wider, within the bound.
A program may use at most 128 MiB of HBM per device.

```python
import jax
import jax.numpy as jnp
from jax import lax

C1 = 64
C2 = 128
PXY = 16
PZ = 4
SLOTS = 3
SLABS = 4
SLOTS_ALL = 24
NP = 16
CELLS = 1024
CELLS_TWO = 128
N_DP = 4
N_SPACE = 8


def draw_patch_home(key, part):
    pair_count = N_SPACE // 2
    first_counts = jax.random.randint(jax.random.fold_in(key, 11), (pair_count,), 1, SLOTS + 1)
    first_counts = first_counts.at[0].set(SLOTS).at[pair_count - 1].set(1)
    counts = jnp.stack([first_counts, SLOTS + 1 - first_counts], axis=1).reshape(N_SPACE)
    starts = jnp.cumsum(counts) - counts
    patch_ids = jnp.arange(NP, dtype=jnp.int32)
    device = jnp.sum((starts[None, :] <= patch_ids[:, None]).astype(jnp.int32), axis=1) - 1
    rank_in = patch_ids - starts[device]
    subkeys = jax.random.split(jax.random.fold_in(key, 12), N_SPACE)
    orders = jax.vmap(lambda subkey: jax.random.permutation(subkey, SLOTS))(subkeys)
    slot_ids = orders[device, rank_in]
    return (device * SLOTS + slot_ids).astype(jnp.int32)


def draw_patch_links(key, part):
    row_count = NP // 2
    cross = jax.random.randint(jax.random.fold_in(key, 21), (row_count,), 0, 4) > 0
    cross = cross.at[0].set(True).at[row_count - 1].set(True)
    upward = jax.random.randint(jax.random.fold_in(key, 22), (row_count - 1, 2), 0, 4) > 0
    none_row = jnp.zeros((1, 2), dtype=jnp.bool_)
    below = jnp.concatenate([none_row, upward], axis=0)
    above = jnp.concatenate([upward, none_row], axis=0)
    row_index = jnp.arange(row_count, dtype=jnp.int32)[:, None]
    column = jnp.arange(2, dtype=jnp.int32)[None, :]
    patch_ids = 2 * row_index + column
    minus_x = jnp.where((column == 1) & cross[:, None], patch_ids - 1, -1)
    plus_x = jnp.where((column == 0) & cross[:, None], patch_ids + 1, -1)
    minus_y = jnp.where(below, patch_ids - 2, -1)
    plus_y = jnp.where(above, patch_ids + 2, -1)
    return jnp.stack([minus_x, plus_x, minus_y, plus_y], axis=-1).reshape(NP, 4).astype(jnp.int32)


def level_of(key, dims, cuts, low, high):
    loudness = 1.0
    for axis_at, parts in cuts:
        steps = jax.random.uniform(jax.random.fold_in(jax.random.fold_in(key, 6), axis_at), (parts,), jnp.float32, low / len(cuts), high / len(cuts))
        loudness = loudness * jnp.repeat(jnp.exp(steps), dims[axis_at] // parts).reshape((-1,) + (1,) * (len(dims) - 1 - axis_at))
    return loudness


def scatter_about(own_key, dims, deviation, reach, cuts=(), kind=jnp.bfloat16):
    array = deviation * jax.random.normal(own_key, dims, jnp.float32)
    if cuts:
        array = array * level_of(own_key, dims, cuts, -0.22, 0.18)
    return jnp.clip(array, -reach, reach).astype(kind)


def setup_inputs(seed: int = 0) -> dict:
    key_of = jax.random.split(jax.random.key(seed), 8)
    return {
        "features": scatter_about(key_of[0], (SLABS, SLOTS_ALL, C1, CELLS), 1.0, 6.0, ((0, 4), (1, 8))),
        "cotangent": scatter_about(key_of[1], (SLABS, SLOTS_ALL, C2, CELLS_TWO), 1.0, 6.0, ((0, 4), (1, 8))),
        "conv_one": scatter_about(key_of[2], (C1, 27 * C1), (27 * C1) ** -0.5, 0.15625, ((0, 4),)),
        "down_weight": scatter_about(key_of[3], (C2, 8 * C1), (8 * C1) ** -0.5, 0.25, ((0, 4),)),
        "conv_two": scatter_about(key_of[4], (C2, 27 * C2), (27 * C2) ** -0.5, 0.109375, ((0, 4),)),
        "patch_home": draw_patch_home(jax.random.fold_in(key_of[7], 71), 0),
        "patch_links": draw_patch_links(jax.random.fold_in(key_of[7], 71), 0),
    }


def slope_of(values):
    logistic = jax.nn.sigmoid(values)
    return logistic * (1.0 + values * (1.0 - logistic))

def neighbour_of(source, linkage, column):
    target = linkage[:, column]
    taken_all = jnp.take(source, jnp.maximum(target, 0), axis=0)
    return jnp.where((target >= 0)[:, None, None, None, None], taken_all, jnp.zeros_like(taken_all))

def assemble(field, linkage):
    lower_rim = neighbour_of(field, linkage, 0)[:, :, -1:]
    upper_rim = neighbour_of(field, linkage, 1)[:, :, :1]
    widened = jnp.concatenate([lower_rim, field, upper_rim], axis=2)
    front_rim = neighbour_of(widened, linkage, 2)[:, :, :, -1:]
    back_rim = neighbour_of(widened, linkage, 3)[:, :, :, :1]
    full_block = jnp.concatenate([front_rim, widened, back_rim], axis=3)
    return jnp.pad(full_block, ((0, 0), (0, 0), (0, 0), (0, 0), (1, 1)))

def convolve(padded, kernel_weight):
    channels = padded.shape[1]
    kernel = kernel_weight.reshape(kernel_weight.shape[0], 3, 3, 3, channels).transpose(0, 4, 1, 2, 3)
    return lax.conv_general_dilated(padded, kernel, (1, 1, 1), 'VALID', dimension_numbers=('NCDHW', 'OIDHW', 'NCDHW'), precision=lax.Precision.HIGHEST)

def coarsen_grid(hidden_state, kernel_weight):
    number, channels, size_x, size_y, size_z = hidden_state.shape
    kernel = kernel_weight.reshape(kernel_weight.shape[0], 2, 2, 2, channels)
    blocks = hidden_state.reshape(number, channels, size_x // 2, 2, size_y // 2, 2, size_z // 2, 2)
    return jnp.einsum('oabcm,nmxaybzc->noxyz', kernel, blocks, precision=lax.Precision.HIGHEST)

def reference(features, cotangent, conv_one, down_weight, conv_two, patch_home, patch_links):
    weight_one = conv_one.astype(jnp.float32)
    coarsen_weight = down_weight.astype(jnp.float32)
    weight_two = conv_two.astype(jnp.float32)
    grad_scale = float(N_DP * NP * (PXY // 2) * (PXY // 2) * (PZ // 2)) ** (-0.5)
    sum_one = jnp.zeros(weight_one.shape, jnp.float32)
    sum_down = jnp.zeros(coarsen_weight.shape, jnp.float32)
    sum_two = jnp.zeros(weight_two.shape, jnp.float32)
    outputs = []
    for slab in range(N_DP):
        patch_field = jnp.take(features[slab], patch_home, axis=0).reshape(NP, C1, PXY, PXY, PZ)
        padded = assemble(patch_field, patch_links).astype(jnp.float32)
        pre_one, back_one = jax.vjp(lambda kernel_weight: convolve(padded, kernel_weight), weight_one)
        hidden_state = jax.nn.silu(pre_one).astype(jnp.bfloat16)
        hidden_state_wide = lax.optimization_barrier(hidden_state).astype(jnp.float32)
        channel_reduced_sum, reverse_downward = jax.vjp(coarsen_grid, hidden_state_wide, coarsen_weight)
        reduced = channel_reduced_sum.astype(jnp.bfloat16)
        reduced_wide = lax.optimization_barrier(reduced).astype(jnp.float32)
        padded_two, back_gather = jax.vjp(lambda values: assemble(values, patch_links), reduced_wide)
        pre_two, back_two = jax.vjp(convolve, padded_two, weight_two)
        activated = jax.nn.silu(pre_two).astype(jnp.bfloat16)
        placed = jnp.zeros((N_SPACE * SLOTS, C2, CELLS_TWO), jnp.bfloat16)
        placed = placed.at[patch_home].set(activated.reshape(NP, C2, CELLS_TWO))
        outputs.append(placed)
        incoming = jnp.take(cotangent[slab], patch_home, axis=0).reshape(pre_two.shape).astype(jnp.float32)
        grad_two = (incoming * slope_of(pre_two) * grad_scale).astype(jnp.bfloat16)
        grad_padded, dw_two = back_two(lax.optimization_barrier(grad_two).astype(jnp.float32))
        grad_reduced_sum, = back_gather(grad_padded)
        grad_reduced = grad_reduced_sum.astype(jnp.bfloat16)
        grad_hidden, dw_down = reverse_downward(lax.optimization_barrier(grad_reduced).astype(jnp.float32))
        grad_one = (grad_hidden * slope_of(pre_one)).astype(jnp.bfloat16)
        dw_one, = back_one(lax.optimization_barrier(grad_one).astype(jnp.float32))
        sum_one = sum_one + dw_one
        sum_down = sum_down + dw_down
        sum_two = sum_two + dw_two
    return (jnp.stack(outputs), sum_one, sum_down, sum_two)
```

```python
import functools

import jax
import jax.numpy as jnp
import numpy as np
from jax import lax
from jax.experimental import pallas as pl
from jax.experimental.pallas import tpu as pltpu
from jax.sharding import PartitionSpec as P

PXY = 16
PZ = 4
LEAD = 8
BF = jnp.bfloat16
F32 = jnp.float32
MESH = pl.DeviceIdType.MESH
VM = pl.BlockSpec(memory_space=pltpu.VMEM)
SM = pl.BlockSpec(memory_space=pltpu.SMEM)
BIG = 58 * 1024 * 1024


def up128(value):
    return -(-value // 128) * 128


def dot(a, b):
    return jnp.dot(a, b, preferred_element_type=F32)


def dot_nt(a, b):
    return lax.dot_general(a, b, (((1,), (1,)), ((), ())), preferred_element_type=F32)


def sigmoid(v):
    return 1.0 / (1.0 + jnp.exp(-v))


def onehot(rows, cols, pairs):
    m = np.zeros((rows, cols), np.float32)
    for r, c in pairs:
        m[r, c] = 1.0
    return jnp.asarray(m, BF)


class Level:
    def __init__(self, xy, z):
        self.xy, self.z = xy, z
        self.yz = xy * z
        self.cells = xy * xy * z
        self.stride = (xy + 2) * z
        self.out = up128(xy * self.stride)
        self.wide = up128(LEAD + self.out + 2 * self.stride + z + 1)

    def cell(self, x, y, k):
        return x * self.yz + y * self.z + k

    def pad(self, x, y, k):
        return LEAD + (x + 1) * self.stride + (y + 1) * self.z + k

    def pos(self, x, y, k):
        return x * self.stride + (y + 1) * self.z + k

    def shift(self, tap):
        dx, dy, dz = tap // 9 - 1, (tap // 3) % 3 - 1, tap % 3 - 1
        return LEAD + self.stride * (1 + dx) + self.z * dy + dz

    def all(self):
        r, q = range(self.xy), range(self.z)
        return [(x, y, k) for x in r for y in r for k in q]

    def face_y(self):
        last = self.xy - 1
        r, q = range(self.xy), range(self.z)
        pairs = []
        for x in r:
            for k in q:
                pairs.append((self.cell(x, 0, k), (x + 1) * self.z + k))
                pairs.append((self.cell(x, last, k), 128 + (x + 1) * self.z + k))
        return onehot(self.cells, 256, pairs)

    def rim_to_face_y(self):
        last = self.xy - 1
        pairs = []
        for k in range(self.z):
            for base, xe in ((0, self.xy + 1), (64, 0)):
                pairs.append((base + k, xe * self.z + k))
                pairs.append((base + last * self.z + k, 128 + xe * self.z + k))
        return onehot(128, 256, pairs)

    def place_x(self):
        pairs = []
        for y in range(self.xy):
            for k in range(self.z):
                pairs.append((y * self.z + k, self.pad(self.xy, y, k)))
                pairs.append((64 + y * self.z + k, self.pad(-1, y, k)))
        return onehot(128, self.wide, pairs)

    def place_y(self):
        pairs = []
        for xe in range(self.xy + 2):
            for k in range(self.z):
                pairs.append((xe * self.z + k, self.pad(xe - 1, self.xy, k)))
                pairs.append((128 + xe * self.z + k, self.pad(xe - 1, -1, k)))
        return onehot(256, self.wide, pairs)

    def place(self):
        return onehot(self.cells, self.wide, [(self.cell(*c), self.pad(*c)) for c in self.all()])


def barrier(lists):
    sem = pltpu.get_barrier_semaphore()
    for target in lists:
        pl.semaphore_signal(sem, inc=1, device_id=target, device_id_type=MESH)
    pl.semaphore_wait(sem, len(lists))


def near(n):
    me = lax.axis_index("space")
    return {k: lax.rem(me + k + n, n) for k in (-2, -1, 1, 2)}


def members(n, group):
    me = lax.axis_index("space")
    base = (me // group) * group
    mine = me - base
    return mine, [base + lax.rem(mine + k, group) for k in range(1, group)]


def swap(n, src, dst, reach, send, recv):
    ids = near(n)
    order = [k for k in range(-reach, reach + 1) if k != 0]
    copies = []
    for i, k in enumerate(order):
        copies.append(
            pltpu.make_async_remote_copy(
                src_ref=src,
                dst_ref=dst.at[i],
                send_sem=send.at[i],
                recv_sem=recv.at[i],
                device_id={"space": ids[-k]},
                device_id_type=MESH,
            )
        )
    for c in copies:
        c.start()
    return order, copies


def select(sel_ref, slots, own, got, order, upper, lower):
    width = own.shape[2]
    first = lax.broadcasted_iota(jnp.int32, (1, width), 1) < width // 2
    blocks = [(k, s, (own[s] if k == 0 else got[order.index(k), s]).astype(F32))
              for k in [0] + order for s in range(slots)]
    result = []
    for t in range(slots):
        total = None
        for k, s, block in blocks:
            at = lambda side: sel_ref[((side * slots + t) * 5 + k + 2) * slots + s]
            term = block * jnp.where(first, at(upper), at(lower))
            total = term if total is None else total + term
        result.append(total.astype(BF))
    return result


def halo_body(n, lv, slots, field, sel, e_face, e_rim, rx, ry, sx, sy, gx, gy, xs, xr, ys, yr):
    chan = field.shape[1]
    last = lv.cells - lv.yz
    sx[...] = jnp.zeros_like(sx)
    sx[:, :, 0 : lv.yz] = field[:, :, 0 : lv.yz]
    sx[:, :, 64 : 64 + lv.yz] = field[:, :, last : lv.cells]
    order, copies = swap(n, sx, gx, 1, xs, xr)
    base = dot(field[...].reshape(slots * chan, lv.cells), e_face[...])
    for c in copies:
        c.wait()
    rims = select(sel, slots, sx, gx, order, 1, 0)
    for s in range(slots):
        rx[s] = rims[s]
        sy[s] = (base[s * chan : (s + 1) * chan] + dot(rims[s], e_rim[...])).astype(BF)
    order, copies = swap(n, sy, gy, 2, ys, yr)
    for c in copies:
        c.wait()
    rims = select(sel, slots, sy, gy, order, 3, 2)
    for s in range(slots):
        ry[s] = rims[s]


def halo_scratch(slots, chan):
    return [
        pltpu.VMEM((slots, chan, 128), BF),
        pltpu.VMEM((slots, chan, 256), BF),
        pltpu.VMEM((2, slots, chan, 128), BF),
        pltpu.VMEM((4, slots, chan, 256), BF),
        pltpu.SemaphoreType.DMA((2,)),
        pltpu.SemaphoreType.DMA((2,)),
        pltpu.SemaphoreType.DMA((4,)),
        pltpu.SemaphoreType.DMA((4,)),
    ]


class Pack:
    def __init__(self, one, down, two, group):
        self.one, self.down, self.two = one, down, two
        self.rows = two[0]
        self.half = up128(-(-one[1] // 2))
        self.at_down = two[1]
        self.at_one = two[1] + down[1]
        self.total = -(-(self.at_one + self.half) // (group * 128)) * group * 128
        self.part = self.total // group
        self.rest = one[1] - self.half

    def put(self, dst, one, down, two):
        low = self.one[0]
        a = self.at_one
        dst[:, 0 : self.at_down] = two
        dst[:, self.at_down : a] = down
        dst[:, a:] = jnp.zeros((self.rows, self.total - a), dst.dtype)
        dst[0:low, a : a + self.half] = one[:, 0 : self.half]
        dst[low : 2 * low, a : a + self.rest] = one[:, self.half :]

    def lanes(self, index):
        return pl.ds(pl.multiple_of(index * self.part, 128), self.part)


def start_kernel(n, dps, group, lv, slots, pack, field, sel, e_face, e_rim, one, down, two, rx, ry, full,
                 packed, gath, zs, zr, ms, mr, *halo):
    dp = lax.axis_index("dp")
    mine, others = members(n, group)
    peers = [lax.rem(dp + k, dps) for k in range(1, dps)]
    pack.put(packed, one[...], down[...], two[...])
    barrier([{"space": t} for t in near(n).values()] + [{"space": t} for t in others]
            + [{"dp": t} for t in peers])
    lanes = pack.lanes(mine)
    zc = []
    for i, t in enumerate(peers):
        zc.append(pltpu.make_async_remote_copy(
            src_ref=packed.at[:, lanes], dst_ref=gath.at[dp, :, lanes],
            send_sem=zs.at[i], recv_sem=zr.at[i], device_id={"dp": t}, device_id_type=MESH))
    for c in zc:
        c.start()
    gath[dp] = packed[...]
    mc = []
    for i in range(dps - 1):
        zc[i].wait()
        source = lax.rem(dp + dps - 1 - i, dps)
        for j, t in enumerate(others):
            c = pltpu.make_async_remote_copy(
                src_ref=gath.at[source, :, lanes], dst_ref=gath.at[source, :, lanes],
                send_sem=ms.at[i, j], recv_sem=mr.at[i, j], device_id={"space": t}, device_id_type=MESH)
            c.start()
            mc.append((c, i, j))
    halo_body(n, lv, slots, field, sel, e_face, e_rim, rx, ry, *halo)
    for c, i, j in mc:
        c.wait()
    full[...] = gath[...]


def halo_kernel(n, lv, slots, field, sel, e_face, e_rim, rx, ry, *halo):
    barrier([{"space": t} for t in near(n).values()])
    halo_body(n, lv, slots, field, sel, e_face, e_rim, rx, ry, *halo)


def columns(lv, padded, chan, store):
    lane = lax.broadcasted_iota(jnp.int32, padded.shape, 1) % lv.z
    zero = jnp.zeros_like(padded)
    kinds = [jnp.where(lane == lv.z - 1, zero, padded), padded, jnp.where(lane == 0, zero, padded)]
    for tap in range(27):
        a = lv.shift(tap)
        store(tap, kinds[tap % 3][:, a : a + lv.out])


def unfold_one(pack, dps, full, w1):
    low = pack.one[0]
    a = pack.at_one
    for d in range(dps):
        w1[d * low : (d + 1) * low, 0 : pack.half] = full[d, 0:low, a : a + pack.half]
        w1[d * low : (d + 1) * low, pack.half :] = full[d, low : 2 * low, a : a + pack.rest]


def first_kernel(lv, slots, pack, dps, field, rx, ry, e_place, e_x, e_y, e_perm, full,
                 padded, pre, split, reduced, w1, xcol):
    chan = field.shape[1]
    unfold_one(pack, dps, full, w1)
    rows = slots * chan
    pad = (dot(field[...].reshape(rows, lv.cells), e_place[...])
           + dot(rx[...].reshape(rows, 128), e_x[...])
           + dot(ry[...].reshape(rows, 256), e_y[...])).astype(BF)
    down = full[:, :, pack.at_down : pack.at_one].reshape(dps * pack.rows, pack.down[1])
    cells = lv.cells // 8
    for s in range(slots):
        mine = pad[s * chan : (s + 1) * chan]
        padded[s] = mine

        def store(tap, value):
            xcol[tap * chan : (tap + 1) * chan] = value

        columns(lv, mine, chan, store)
        value = dot(w1[...], xcol[...])
        pre[s] = value
        hidden = (value * sigmoid(value)).astype(BF)
        parts = dot(hidden, e_perm[...]).astype(BF)
        stacked = jnp.concatenate([parts[:, e * cells : (e + 1) * cells] for e in range(8)], axis=0)
        split[s] = stacked
        reduced[s] = dot(down, stacked).astype(BF)


def second_kernel(lv, slots, pack, dps, scale, field, rx, ry, e_place, e_x, e_y, e_trim, e_spread, cot, live, full,
                  level, dw, gp, xcol, gcol, wt, gbuf):
    chan = field.shape[1]
    rows = slots * chan
    pad = (dot(field[...].reshape(rows, lv.cells), e_place[...])
           + dot(rx[...].reshape(rows, 128), e_x[...])
           + dot(ry[...].reshape(rows, 256), e_y[...])).astype(BF)
    w2 = full[:, :, 0 : pack.at_down].reshape(dps * pack.rows, pack.at_down)
    out = lv.out
    for s in range(slots):
        def store(tap, value):
            xcol[tap * chan : (tap + 1) * chan, s * out : (s + 1) * out] = value

        columns(lv, pad[s * chan : (s + 1) * chan], chan, store)
    pre = dot(w2, xcol[...])
    gbuf[...] = jnp.zeros_like(gbuf)
    lane = lax.broadcasted_iota(jnp.int32, (1, out), 1) % lv.z
    grads = []
    for s in range(slots):
        v = pre[:, s * out : (s + 1) * out]
        sg = sigmoid(v)
        act = dot((v * sg).astype(BF), e_trim[...])
        alive = live[s] > 0.5
        level[s] = jnp.where(alive, act, 0.0).astype(BF)
        inc = dot(cot[s], e_spread[...])
        g = jnp.where(alive, inc * (sg * (1.0 + v * (1.0 - sg))) * scale, 0.0)
        grads.append(g.astype(BF))
        for d in range(3):
            keep = lane >= 0 if d == 1 else (lane != 0 if d == 0 else lane != lv.z - 1)
            gbuf[d, :, 128 : 128 + out] = jnp.where(keep, g, 0.0).astype(BF)
        for tap in range(27):
            a = 128 - lv.shift(tap)
            gcol[tap * chan : (tap + 1) * chan, s * out : (s + 1) * out] = gbuf[tap % 3, :, a : a + out]
    for tap in range(27):
        wt[:, tap * chan : (tap + 1) * chan] = w2[:, tap * chan : (tap + 1) * chan].astype(F32).T.astype(BF)
    back = dot(wt[...], gcol[...])
    for s in range(slots):
        gp[s] = back[:, s * out : (s + 1) * out]
    dw[...] = dot_nt(jnp.concatenate(grads, axis=1), xcol[...]).astype(BF)


def back_kernel(n, lv, slots, gp, sel, e_gy, e_by, e_gx, e_dense, e_bx, out,
                sx, sy, gx, gy, xs, xr, ys, yr):
    barrier([{"space": t} for t in near(n).values()])
    for s in range(slots):
        sy[s] = dot(gp[s].astype(BF), e_gy[...]).astype(BF)
    order, copies = swap(n, sy, gy, 2, ys, yr)
    for c in copies:
        c.wait()
    back = select(sel, slots, sy, gy, order, 3, 2)
    dense = []
    for s in range(slots):
        w = gp[s] + dot(back[s], e_by[...])
        hi = w.astype(BF)
        low = (w - hi.astype(F32)).astype(BF)
        sx[s] = dot(hi, e_gx[...]).astype(BF)
        dense.append(dot(hi, e_dense[...]) + dot(low, e_dense[...]))
    order, copies = swap(n, sx, gx, 1, xs, xr)
    for c in copies:
        c.wait()
    back = select(sel, slots, sx, gx, order, 1, 0)
    for s in range(slots):
        out[s] = (dense[s] + dot(back[s], e_bx[...])).astype(BF)


def last_kernel(lv, slots, pack, dps, gr, split, pre, padded, e_up, kind, full, dw_one, dw_down, xcol):
    chan = pre.shape[1]
    down = full[:, :, pack.at_down : pack.at_one].reshape(dps * pack.rows, pack.down[1])
    down_t = down.astype(F32).T.astype(BF)
    total_down = None
    total_one = None
    for s in range(slots):
        g = gr[s]
        part = dot_nt(g, split[s])
        total_down = part if total_down is None else total_down + part
        up = dot(g, e_up[...]).astype(BF)
        eight = dot(down_t, up)
        gh = None
        for e in range(8):
            term = jnp.where(kind[...] == e, eight[e * chan : (e + 1) * chan], 0.0)
            gh = term if gh is None else gh + term
        v = pre[s]
        sg = sigmoid(v)
        g1 = (gh * (sg * (1.0 + v * (1.0 - sg)))).astype(BF)

        def store(tap, value):
            xcol[tap * chan : (tap + 1) * chan] = value

        columns(lv, padded[s], chan, store)
        part = dot_nt(g1, xcol[...])
        total_one = part if total_one is None else total_one + part
    dw_down[...] = total_down.astype(BF)
    dw_one[...] = total_one.astype(BF)


def reduce_kernel(n, dps, group, pack, one, down, two, o_one, o_down, o_two,
                  packed, rs, acc, zb, fin, ms, mr, zs, zr, fs, fr):
    dp = lax.axis_index("dp")
    mine, others = members(n, group)
    me = lax.axis_index("space")
    base = me - mine
    peers = [lax.rem(dp + k, dps) for k in range(1, dps)]
    r1, r2 = pack.one[0], pack.rows
    for d in range(dps):
        pack.put(packed.at[d], one[d * r1 : (d + 1) * r1], down[d * r2 : (d + 1) * r2], two[d * r2 : (d + 1) * r2])
    barrier([{"space": t} for t in others] + [{"dp": t} for t in peers])
    lanes = pack.lanes(mine)
    copies = []
    for j, t in enumerate(others):
        c = pltpu.make_async_remote_copy(
            src_ref=packed.at[:, :, pack.lanes(t - base)], dst_ref=rs.at[j],
            send_sem=ms.at[j], recv_sem=mr.at[j], device_id={"space": t}, device_id_type=MESH)
        c.start()
        copies.append(c)
    total = packed[:, :, lanes].astype(F32)
    for j, c in enumerate(copies):
        c.wait()
        total = total + rs[j].astype(F32)
    acc[...] = total.astype(BF)
    copies = []
    for j, t in enumerate(peers):
        c = pltpu.make_async_remote_copy(
            src_ref=acc.at[t], dst_ref=zb.at[j],
            send_sem=zs.at[j], recv_sem=zr.at[j], device_id={"dp": t}, device_id_type=MESH)
        c.start()
        copies.append(c)
    total = acc[dp].astype(F32)
    for j, c in enumerate(copies):
        c.wait()
        total = total + zb[j].astype(F32)
    fin[:, lanes] = total.astype(BF)
    copies = []
    for j, t in enumerate(others):
        c = pltpu.make_async_remote_copy(
            src_ref=fin.at[:, lanes], dst_ref=fin.at[:, lanes],
            send_sem=fs.at[j], recv_sem=fr.at[j], device_id={"space": t}, device_id_type=MESH)
        c.start()
        copies.append(c)
    for c in copies:
        c.wait()
    a = pack.at_one
    o_two[...] = fin[:, 0 : pack.at_down].astype(F32)
    o_down[...] = fin[:, pack.at_down : a].astype(F32)
    o_one[:, 0 : pack.half] = fin[0:r1, a : a + pack.half].astype(F32)
    o_one[:, pack.half :] = fin[r1 : 2 * r1, a : a + pack.rest].astype(F32)


def call(body, args, specs, outs, scratch, ident=None):
    extra = {} if ident is None else {"collective_id": ident, "has_side_effects": True}
    return pl.pallas_call(
        body,
        out_shape=[jax.ShapeDtypeStruct(s, t) for s, t in outs],
        in_specs=specs,
        out_specs=[VM] * len(outs),
        scratch_shapes=scratch,
        compiler_params=pltpu.CompilerParams(vmem_limit_bytes=BIG, **extra),
    )(*args)


def on_device(features, cotangent, conv_one, down_weight, conv_two, patch_home, patch_links):
    n, dps = lax.axis_size("space"), lax.axis_size("dp")
    group = 8 if n % 8 == 0 else n
    slots, c1 = features.shape[1], features.shape[2]
    c2 = conv_two.shape[0] * dps
    me = lax.axis_index("space")
    one, two = Level(PXY, PZ), Level(PXY // 2, PZ // 2)
    pack = Pack(conv_one.shape, down_weight.shape, conv_two.shape, group)

    own = patch_home[None, :] == (me * slots + jnp.arange(slots, dtype=jnp.int32))[:, None]
    live = jnp.any(own, axis=1).astype(F32)
    ids = jnp.arange(patch_home.shape[0], dtype=jnp.int32)
    codes = (me - 2) * slots + jnp.arange(5 * slots, dtype=jnp.int32)
    target = jnp.max(jnp.where(own[:, :, None], patch_links[None], -1), axis=1)
    source = jnp.max(jnp.where(target[:, :, None] == ids, patch_home, -1), axis=2)
    sel = ((source.T[:, :, None] == codes) & (source.T[:, :, None] >= 0)).astype(F32).reshape(-1)

    field = features[0]
    dma = pltpu.SemaphoreType.DMA
    rx, ry, full = call(
        functools.partial(start_kernel, n, dps, group, one, slots, pack),
        (field, sel, one.face_y(), one.rim_to_face_y(), conv_one, down_weight, conv_two),
        [VM, SM, VM, VM, VM, VM, VM],
        [((slots, c1, 128), BF), ((slots, c1, 256), BF), ((dps, pack.rows, pack.total), BF)],
        [pltpu.VMEM((pack.rows, pack.total), BF), pltpu.VMEM((dps, pack.rows, pack.total), BF),
         dma((dps - 1,)), dma((dps - 1,)), dma((dps - 1, group - 1)), dma((dps - 1, group - 1))]
        + halo_scratch(slots, c1),
        0,
    )

    cells_two = two.cells
    perm = []
    spot = []
    kind = np.full((1, one.out), -1, np.int32)
    for x, y, k in one.all():
        e = (x % 2) * 4 + (y % 2) * 2 + k % 2
        small = two.cell(x // 2, y // 2, k // 2)
        at = one.pos(x, y, k)
        perm.append((at, e * cells_two + small))
        spot.append((small, at))
        kind[0, at] = e
    padded, pre, split, reduced = call(
        functools.partial(first_kernel, one, slots, pack, dps),
        (field, rx, ry, one.place(), one.place_x(), one.place_y(), onehot(one.out, one.cells, perm), full),
        [VM] * 8,
        [((slots, c1, one.wide), BF), ((slots, c1, one.out), F32), ((slots, 8 * c1, cells_two), BF),
         ((slots, c2, cells_two), BF)],
        [pltpu.VMEM((c1, conv_one.shape[1]), BF), pltpu.VMEM((27 * c1, one.out), BF)],
    )

    rx2, ry2 = call(
        functools.partial(halo_kernel, n, two, slots),
        (reduced, sel, two.face_y(), two.rim_to_face_y()),
        [VM, SM, VM, VM],
        [((slots, c2, 128), BF), ((slots, c2, 256), BF)],
        halo_scratch(slots, c2),
        1,
    )

    scale = float(dps * patch_links.shape[0] * cells_two) ** (-0.5)
    trim = [(two.pos(*c), two.cell(*c)) for c in two.all()]
    level, dw_two, gp = call(
        functools.partial(second_kernel, two, slots, pack, dps, scale),
        (reduced, rx2, ry2, two.place(), two.place_x(), two.place_y(), onehot(two.out, cells_two, trim),
         onehot(cells_two, two.out, [(b, a) for a, b in trim]), cotangent[0], live, full),
        [VM] * 9 + [SM, VM],
        [((slots, c2, cells_two), BF), ((c2, 27 * c2), BF), ((slots, c2, two.out), F32)],
        [pltpu.VMEM((27 * c2, slots * two.out), BF), pltpu.VMEM((27 * c2, slots * two.out), BF),
         pltpu.VMEM((c2, 27 * c2), BF), pltpu.VMEM((3, c2, 256 + two.out), BF)],
    )

    last = two.xy - 1
    g_y, b_y, g_x, b_x = [], [], [], []
    for k in range(two.z):
        for xe in range(two.xy + 2):
            lane = xe * two.z + k
            g_y += [(two.pad(xe - 1, -1, k), lane), (two.pad(xe - 1, two.xy, k), 128 + lane)]
            b_y += [(lane, two.pad(xe - 1, last, k)), (128 + lane, two.pad(xe - 1, 0, k))]
        for y in range(two.xy):
            lane = y * two.z + k
            g_x += [(two.pad(-1, y, k), lane), (two.pad(two.xy, y, k), 64 + lane)]
            b_x += [(lane, two.cell(last, y, k)), (64 + lane, two.cell(0, y, k))]
    dense = [(two.pad(*c), two.cell(*c)) for c in two.all()]
    [gr] = call(
        functools.partial(back_kernel, n, two, slots),
        (gp, sel, onehot(two.out, 256, g_y), onehot(256, two.out, b_y), onehot(two.out, 128, g_x),
         onehot(two.out, cells_two, dense), onehot(128, cells_two, b_x)),
        [VM, SM, VM, VM, VM, VM, VM],
        [((slots, c2, cells_two), BF)],
        halo_scratch(slots, c2),
        2,
    )

    dw_one, dw_down = call(
        functools.partial(last_kernel, one, slots, pack, dps),
        (gr, split, pre, padded, onehot(cells_two, one.out, spot), jnp.asarray(kind), full),
        [VM] * 7,
        [((c1, 27 * c1), BF), ((c2, 8 * c1), BF)],
        [pltpu.VMEM((27 * c1, one.out), BF)],
    )

    outs = call(
        functools.partial(reduce_kernel, n, dps, group, pack),
        (dw_one, dw_down, dw_two),
        [VM] * 3,
        [(conv_one.shape, F32), (down_weight.shape, F32), (conv_two.shape, F32)],
        [pltpu.VMEM((dps, pack.rows, pack.total), BF), pltpu.VMEM((group - 1, dps, pack.rows, pack.part), BF),
         pltpu.VMEM((dps, pack.rows, pack.part), BF), pltpu.VMEM((dps - 1, pack.rows, pack.part), BF),
         pltpu.VMEM((pack.rows, pack.total), BF),
         dma((group - 1,)), dma((group - 1,)), dma((dps - 1,)), dma((dps - 1,)), dma((group - 1,)), dma((group - 1,))],
        3,
    )
    if n > group:
        rings = [[a + m for a in range(0, n, group)] for m in range(group)]
        outs = [lax.psum(o, "space", axis_index_groups=rings) for o in outs]
    return (level[None], outs[0], outs[1], outs[2])


def solution(mesh):
    weights = P("dp", None)
    slabs = P("dp", "space", None, None)
    return jax.shard_map(
        on_device,
        mesh=mesh,
        in_specs=(slabs, slabs, weights, weights, weights, P(), P()),
        out_specs=(slabs, weights, weights, weights),
        check_vma=False,
    )
```

```python
import functools

import jax
import jax.numpy as jnp
import numpy as np
from jax import lax
from jax.experimental import pallas as pl
from jax.experimental.pallas import tpu as pltpu
from jax.sharding import PartitionSpec as P

PXY = 16
PZ = 4
LEAD = 8
BF = jnp.bfloat16
F32 = jnp.float32
MESH = pl.DeviceIdType.MESH
VM = pl.BlockSpec(memory_space=pltpu.VMEM)
SM = pl.BlockSpec(memory_space=pltpu.SMEM)
BIG = 58 * 1024 * 1024


def up128(value):
    return -(-value // 128) * 128


def dot(a, b):
    return jnp.dot(a, b, preferred_element_type=F32)


def dot_nt(a, b):
    return lax.dot_general(a, b, (((1,), (1,)), ((), ())), preferred_element_type=F32)


def sigmoid(v):
    return 1.0 / (1.0 + jnp.exp(-v))


def onehot(rows, cols, pairs):
    m = np.zeros((rows, cols), np.float32)
    for r, c in pairs:
        m[r, c] = 1.0
    return jnp.asarray(m, BF)


class Level:
    def __init__(self, xy, z):
        self.xy, self.z = xy, z
        self.yz = xy * z
        self.cells = xy * xy * z
        self.stride = (xy + 2) * z
        self.out = up128(xy * self.stride)
        self.wide = up128(LEAD + self.out + 2 * self.stride + z + 1)

    def cell(self, x, y, k):
        return x * self.yz + y * self.z + k

    def pad(self, x, y, k):
        return LEAD + (x + 1) * self.stride + (y + 1) * self.z + k

    def pos(self, x, y, k):
        return x * self.stride + (y + 1) * self.z + k

    def shift(self, tap):
        dx, dy, dz = tap // 9 - 1, (tap // 3) % 3 - 1, tap % 3 - 1
        return LEAD + self.stride * (1 + dx) + self.z * dy + dz

    def all(self):
        r, q = range(self.xy), range(self.z)
        return [(x, y, k) for x in r for y in r for k in q]

    def face_y(self):
        last = self.xy - 1
        r, q = range(self.xy), range(self.z)
        pairs = []
        for x in r:
            for k in q:
                pairs.append((self.cell(x, 0, k), (x + 1) * self.z + k))
                pairs.append((self.cell(x, last, k), 128 + (x + 1) * self.z + k))
        return onehot(self.cells, 256, pairs)

    def rim_to_face_y(self):
        last = self.xy - 1
        pairs = []
        for k in range(self.z):
            for base, xe in ((0, self.xy + 1), (64, 0)):
                pairs.append((base + k, xe * self.z + k))
                pairs.append((base + last * self.z + k, 128 + xe * self.z + k))
        return onehot(128, 256, pairs)

    def place_x(self):
        pairs = []
        for y in range(self.xy):
            for k in range(self.z):
                pairs.append((y * self.z + k, self.pad(self.xy, y, k)))
                pairs.append((64 + y * self.z + k, self.pad(-1, y, k)))
        return onehot(128, self.wide, pairs)

    def place_y(self):
        pairs = []
        for xe in range(self.xy + 2):
            for k in range(self.z):
                pairs.append((xe * self.z + k, self.pad(xe - 1, self.xy, k)))
                pairs.append((128 + xe * self.z + k, self.pad(xe - 1, -1, k)))
        return onehot(256, self.wide, pairs)

    def place(self):
        return onehot(self.cells, self.wide, [(self.cell(*c), self.pad(*c)) for c in self.all()])


def barrier(lists):
    sem = pltpu.get_barrier_semaphore()
    for target in lists:
        pl.semaphore_signal(sem, inc=1, device_id=target, device_id_type=MESH)
    pl.semaphore_wait(sem, len(lists))


def near(n):
    me = lax.axis_index("space")
    return {k: lax.rem(me + k + n, n) for k in (-2, -1, 1, 2)}


def members(n, group):
    me = lax.axis_index("space")
    inside = lax.rem(me, group)
    base = me - inside
    core, chip = lax.rem(inside, 2), inside // 2
    chips = group // 2
    others = [lax.rem(chip + k, chips) for k in range(1, chips)]
    return core, chip, base + 2 * chip + 1 - core, others, [base + 2 * t + core for t in others]


def swap(n, src, dst, reach, send, recv):
    ids = near(n)
    order = [k for k in range(-reach, reach + 1) if k != 0]
    copies = []
    for i, k in enumerate(order):
        copies.append(
            pltpu.make_async_remote_copy(
                src_ref=src,
                dst_ref=dst.at[i],
                send_sem=send.at[i],
                recv_sem=recv.at[i],
                device_id={"space": ids[-k]},
                device_id_type=MESH,
            )
        )
    for c in copies:
        c.start()
    return order, copies


def select(sel_ref, slots, own, got, order, upper, lower):
    width = own.shape[2]
    first = lax.broadcasted_iota(jnp.int32, (1, width), 1) < width // 2
    blocks = [(k, s, (own[s] if k == 0 else got[order.index(k), s]).astype(F32))
              for k in [0] + order for s in range(slots)]
    result = []
    for t in range(slots):
        total = None
        for k, s, block in blocks:
            at = lambda side: sel_ref[((side * slots + t) * 5 + k + 2) * slots + s]
            term = block * jnp.where(first, at(upper), at(lower))
            total = term if total is None else total + term
        result.append(total.astype(BF))
    return result


def halo_body(n, lv, slots, field, sel, e_face, e_rim, rx, ry, sx, sy, gx, gy, xs, xr, ys, yr, between):
    chan = field.shape[1]
    last = lv.cells - lv.yz
    sx[...] = jnp.zeros_like(sx)
    sx[:, :, 0 : lv.yz] = field[:, :, 0 : lv.yz]
    sx[:, :, 64 : 64 + lv.yz] = field[:, :, last : lv.cells]
    order, copies = swap(n, sx, gx, 1, xs, xr)
    base = dot(field[...].reshape(slots * chan, lv.cells), e_face[...])
    for c in copies:
        c.wait()
    rims = select(sel, slots, sx, gx, order, 1, 0)
    for s in range(slots):
        rx[s] = rims[s]
        sy[s] = (base[s * chan : (s + 1) * chan] + dot(rims[s], e_rim[...])).astype(BF)
    order, copies = swap(n, sy, gy, 2, ys, yr)
    between()
    for c in copies:
        c.wait()
    rims = select(sel, slots, sy, gy, order, 3, 2)
    for s in range(slots):
        ry[s] = rims[s]


def halo_scratch(slots, chan):
    return [
        pltpu.VMEM((slots, chan, 128), BF),
        pltpu.VMEM((slots, chan, 256), BF),
        pltpu.VMEM((2, slots, chan, 128), BF),
        pltpu.VMEM((4, slots, chan, 256), BF),
        pltpu.SemaphoreType.DMA((2,)),
        pltpu.SemaphoreType.DMA((2,)),
        pltpu.SemaphoreType.DMA((4,)),
        pltpu.SemaphoreType.DMA((4,)),
    ]


class Pack:
    def __init__(self, one, down, two, group):
        self.one, self.down, self.two = one, down, two
        self.rows = two[0]
        self.half = up128(-(-one[1] // 2))
        self.at_down = two[1]
        self.at_one = two[1] + down[1]
        self.total = -(-(self.at_one + self.half) // (group * 128)) * group * 128
        self.part = self.total // group
        self.rest = one[1] - self.half

    def put(self, dst, one, down, two):
        low = self.one[0]
        a = self.at_one
        dst[:, 0 : self.at_down] = two
        dst[:, self.at_down : a] = down
        dst[:, a:] = jnp.zeros((self.rows, self.total - a), dst.dtype)
        dst[0:low, a : a + self.half] = one[:, 0 : self.half]
        dst[low : 2 * low, a : a + self.rest] = one[:, self.half :]

    def lanes(self, index):
        return pl.ds(pl.multiple_of(index * self.part, 128), self.part)


def remote(src, dst, send, recv, target):
    return pltpu.make_async_remote_copy(
        src_ref=src, dst_ref=dst, send_sem=send, recv_sem=recv, device_id=target, device_id_type=MESH
    )


def start_kernel(n, dps, group, lv, slots, pack, field, sel, e_face, e_rim, one, down, two, rx, ry, full,
                 packed, gath, zs, zr, ms, mr, ps, pr, *halo):
    dp = lax.axis_index("dp")
    core, chip, sibling, others, targets = members(n, group)
    chips = group // 2
    peers = [lax.rem(dp + k, dps) for k in range(1, dps)]
    pack.put(packed, one[...], down[...], two[...])
    barrier([{"space": t} for t in near(n).values()] + [{"space": t} for t in targets + [sibling]]
            + [{"dp": t} for t in peers])
    lanes = pack.lanes(core * chips + chip)
    zc = []
    for i, t in enumerate(peers):
        zc.append(remote(packed.at[:, lanes], gath.at[dp, :, lanes], zs.at[i], zr.at[i], {"dp": t}))
    for c in zc:
        c.start()
    gath[dp] = packed[...]
    mc, sc = [], []
    shares = [lax.rem(dp + dps - 1 - i, dps) for i in range(dps - 1)]
    for i in range(dps - 1):
        zc[i].wait()
        block = gath.at[shares[i], :, lanes]
        for j, t in enumerate(targets):
            c = remote(block, block, ms.at[i, j], mr.at[i, j], {"space": t})
            c.start()
            mc.append(c)
        c = remote(block, block, ps.at[i, chips - 1], pr.at[i, chips - 1], {"space": sibling})
        c.start()
        sc.append(c)

    def between():
        for i in range(dps - 1):
            for j in range(chips - 1):
                mc[i * (chips - 1) + j].wait()
                sender = lax.rem(chip + chips - 1 - j, chips)
                block = gath.at[shares[i], :, pack.lanes(core * chips + sender)]
                c = remote(block, block, ps.at[i, j], pr.at[i, j], {"space": sibling})
                c.start()
                sc.append(c)

    halo_body(n, lv, slots, field, sel, e_face, e_rim, rx, ry, *halo, between)
    for c in sc:
        c.wait()
    full[...] = gath[...]


def routed(block, got, order, route):
    total = dot(block[...], route[2])
    for i, k in enumerate(order):
        total = total + dot(got[i], route[k + 2])
    return total.astype(BF)


def halo_kernel(n, lv, slots, field, way_x, way_y, e_x, e_y, e_rim, rx, ry, sx, sy, gx, gy, xs, xr, ys, yr):
    wide = jnp.concatenate([field[s] for s in range(slots)], axis=1)
    sx[...] = dot(wide, e_x[...]).astype(BF)
    barrier([{"space": t} for t in near(n).values()])
    order, copies = swap(n, sx, gx, 1, xs, xr)
    base = dot(wide, e_y[...])
    for c in copies:
        c.wait()
    rim = routed(sx, gx, order, way_x)
    rx[...] = rim
    sy[...] = (base + dot(rim, e_rim[...])).astype(BF)
    order, copies = swap(n, sy, gy, 2, ys, yr)
    for c in copies:
        c.wait()
    ry[...] = routed(sy, gy, order, way_y)


def packed_scratch(chan):
    return [
        pltpu.VMEM((chan, 128), BF),
        pltpu.VMEM((chan, 128), BF),
        pltpu.VMEM((2, chan, 128), BF),
        pltpu.VMEM((4, chan, 128), BF),
        pltpu.SemaphoreType.DMA((2,)),
        pltpu.SemaphoreType.DMA((2,)),
        pltpu.SemaphoreType.DMA((4,)),
        pltpu.SemaphoreType.DMA((4,)),
    ]


def columns(lv, padded, chan, store):
    lane = lax.broadcasted_iota(jnp.int32, padded.shape, 1) % lv.z
    zero = jnp.zeros_like(padded)
    kinds = [jnp.where(lane == lv.z - 1, zero, padded), padded, jnp.where(lane == 0, zero, padded)]
    for tap in range(27):
        a = lv.shift(tap)
        store(tap, kinds[tap % 3][:, a : a + lv.out])


def unfold_one(pack, dps, full, w1):
    low = pack.one[0]
    a = pack.at_one
    for d in range(dps):
        w1[d * low : (d + 1) * low, 0 : pack.half] = full[d, 0:low, a : a + pack.half]
        w1[d * low : (d + 1) * low, pack.half :] = full[d, low : 2 * low, a : a + pack.rest]


def first_kernel(lv, slots, pack, dps, field, rx, ry, e_place, e_x, e_y, e_perm, full,
                 padded, pre, split, reduced, w1, xcol):
    chan = field.shape[1]
    unfold_one(pack, dps, full, w1)
    rows = slots * chan
    pad = (dot(field[...].reshape(rows, lv.cells), e_place[...])
           + dot(rx[...].reshape(rows, 128), e_x[...])
           + dot(ry[...].reshape(rows, 256), e_y[...])).astype(BF)
    down = full[:, :, pack.at_down : pack.at_one].reshape(dps * pack.rows, pack.down[1])
    cells = lv.cells // 8
    for s in range(slots):
        mine = pad[s * chan : (s + 1) * chan]
        padded[s] = mine

        def store(tap, value):
            xcol[tap * chan : (tap + 1) * chan] = value

        columns(lv, mine, chan, store)
        value = dot(w1[...], xcol[...])
        pre[s] = value
        hidden = (value * sigmoid(value)).astype(BF)
        parts = dot(hidden, e_perm[...]).astype(BF)
        stacked = jnp.concatenate([parts[:, e * cells : (e + 1) * cells] for e in range(8)], axis=0)
        split[s] = stacked
        reduced[s] = dot(down, stacked).astype(BF)


def second_kernel(lv, slots, pack, dps, scale, field, rx, ry, e_place, e_x, e_y, e_trim, e_spread, cot, live, full,
                  level, dw, gp, xcol, gcol, wt, gbuf):
    chan = field.shape[1]
    w2 = full[:, :, 0 : pack.at_down].reshape(dps * pack.rows, pack.at_down)
    out = lv.out
    for s in range(slots):
        def store(tap, value):
            xcol[tap * chan : (tap + 1) * chan, s * out : (s + 1) * out] = value

        pad = dot(field[s], e_place[...]) + dot(rx[...], e_x[s]) + dot(ry[...], e_y[s])
        columns(lv, pad.astype(BF), chan, store)
    pre = dot(w2, xcol[...])
    gbuf[...] = jnp.zeros_like(gbuf)
    lane = lax.broadcasted_iota(jnp.int32, (1, out), 1) % lv.z
    grads = []
    for s in range(slots):
        v = pre[:, s * out : (s + 1) * out]
        sg = sigmoid(v)
        act = dot((v * sg).astype(BF), e_trim[...])
        alive = live[s] > 0.5
        level[s] = jnp.where(alive, act, 0.0).astype(BF)
        inc = dot(cot[s], e_spread[...])
        g = jnp.where(alive, inc * (sg * (1.0 + v * (1.0 - sg))) * scale, 0.0)
        grads.append(g.astype(BF))
        for d in range(3):
            keep = lane >= 0 if d == 1 else (lane != 0 if d == 0 else lane != lv.z - 1)
            gbuf[d, :, 128 : 128 + out] = jnp.where(keep, g, 0.0).astype(BF)
        for tap in range(27):
            a = 128 - lv.shift(tap)
            gcol[tap * chan : (tap + 1) * chan, s * out : (s + 1) * out] = gbuf[tap % 3, :, a : a + out]
    for tap in range(27):
        wt[:, tap * chan : (tap + 1) * chan] = w2[:, tap * chan : (tap + 1) * chan].astype(F32).T.astype(BF)
    back = dot(wt[...], gcol[...])
    for s in range(slots):
        gp[s] = back[:, s * out : (s + 1) * out]
    dw[...] = dot_nt(jnp.concatenate(grads, axis=1), xcol[...]).astype(BF)


def back_kernel(n, slots, gp, way_x, way_y, e_gy, e_by, e_gx, e_dense, e_bx, out,
                sx, sy, gx, gy, xs, xr, ys, yr):
    total = None
    for s in range(slots):
        part = dot(gp[s].astype(BF), e_gy[s])
        total = part if total is None else total + part
    sy[...] = total.astype(BF)
    barrier([{"space": t} for t in near(n).values()])
    order, copies = swap(n, sy, gy, 2, ys, yr)
    for c in copies:
        c.wait()
    back = routed(sy, gy, order, way_y)
    dense = []
    total = None
    for s in range(slots):
        w = gp[s] + dot(back, e_by[s])
        hi = w.astype(BF)
        low = (w - hi.astype(F32)).astype(BF)
        part = dot(hi, e_gx[s])
        total = part if total is None else total + part
        dense.append((hi, low))
    sx[...] = total.astype(BF)
    order, copies = swap(n, sx, gx, 1, xs, xr)
    dense = [dot(hi, e_dense[...]) + dot(low, e_dense[...]) for hi, low in dense]
    for c in copies:
        c.wait()
    back = routed(sx, gx, order, way_x)
    for s in range(slots):
        out[s] = (dense[s] + dot(back, e_bx[s])).astype(BF)


def last_kernel(lv, slots, pack, dps, gr, split, pre, padded, e_up, kind, full, dw_one, dw_down, xcol):
    chan = pre.shape[1]
    down = full[:, :, pack.at_down : pack.at_one].reshape(dps * pack.rows, pack.down[1])
    down_t = down.astype(F32).T.astype(BF)
    total_down = None
    total_one = None
    for s in range(slots):
        g = gr[s]
        part = dot_nt(g, split[s])
        total_down = part if total_down is None else total_down + part
        up = dot(g, e_up[...]).astype(BF)
        eight = dot(down_t, up)
        gh = None
        for e in range(8):
            term = jnp.where(kind[...] == e, eight[e * chan : (e + 1) * chan], 0.0)
            gh = term if gh is None else gh + term
        v = pre[s]
        sg = sigmoid(v)
        g1 = (gh * (sg * (1.0 + v * (1.0 - sg)))).astype(BF)

        def store(tap, value):
            xcol[tap * chan : (tap + 1) * chan] = value

        columns(lv, padded[s], chan, store)
        part = dot_nt(g1, xcol[...])
        total_one = part if total_one is None else total_one + part
    dw_down[...] = total_down.astype(BF)
    dw_one[...] = total_one.astype(BF)


def reduce_kernel(n, dps, group, pack, one, down, two, out,
                  packed, r0, a1, rs, acc, zb, fin, ps, pr, ms, mr, zs, zr, fs, fr, qs, qr):
    dp = lax.axis_index("dp")
    core, chip, sibling, others, targets = members(n, group)
    chips = group // 2
    peers = [lax.rem(dp + k, dps) for k in range(1, dps)]
    r1, r2 = pack.one[0], pack.rows
    for d in range(dps):
        pack.put(packed.at[d], one[d * r1 : (d + 1) * r1], down[d * r2 : (d + 1) * r2], two[d * r2 : (d + 1) * r2])
    barrier([{"space": t} for t in targets + [sibling]] + [{"dp": t} for t in peers])
    order = others + [chip]
    copies = []
    for j, t in enumerate(order):
        c = remote(packed.at[:, :, pack.lanes((1 - core) * chips + t)], r0.at[j], ps.at[j], pr.at[j],
                   {"space": sibling})
        c.start()
        copies.append(c)
    sent = []
    for j, t in enumerate(order):
        copies[j].wait()
        value = packed[:, :, pack.lanes(core * chips + t)].astype(F32) + r0[j].astype(F32)
        if j < chips - 1:
            a1[j] = value.astype(BF)
            c = remote(a1.at[j], rs.at[j], ms.at[j], mr.at[j], {"space": targets[j]})
            c.start()
            sent.append(c)
    for j, c in enumerate(sent):
        c.wait()
        value = value + rs[j].astype(F32)
    acc[...] = value.astype(BF)
    copies = []
    for j, t in enumerate(peers):
        c = remote(acc.at[t], zb.at[j], zs.at[j], zr.at[j], {"dp": t})
        c.start()
        copies.append(c)
    total = acc[dp].astype(F32)
    for j, c in enumerate(copies):
        c.wait()
        total = total + zb[j].astype(F32)
    lanes = pack.lanes(core * chips + chip)
    fin[:, lanes] = total.astype(BF)
    block = fin.at[:, lanes]
    copies, last = [], []
    for j, t in enumerate(targets):
        c = remote(block, block, fs.at[j], fr.at[j], {"space": t})
        c.start()
        copies.append(c)
    c = remote(block, block, qs.at[chips - 1], qr.at[chips - 1], {"space": sibling})
    c.start()
    last.append(c)
    for j, c in enumerate(copies):
        c.wait()
        block = fin.at[:, pack.lanes(core * chips + lax.rem(chip + chips - 1 - j, chips))]
        c = remote(block, block, qs.at[j], qr.at[j], {"space": sibling})
        c.start()
        last.append(c)
    for c in last:
        c.wait()
    out[...] = fin[...]


def unfold_kernel(pack, fin, o_one, o_down, o_two):
    r1 = pack.one[0]
    a = pack.at_one
    o_two[...] = fin[:, 0 : pack.at_down].astype(F32)
    o_down[...] = fin[:, pack.at_down : a].astype(F32)
    o_one[:, 0 : pack.half] = fin[0:r1, a : a + pack.half].astype(F32)
    o_one[:, pack.half :] = fin[r1 : 2 * r1, a : a + pack.rest].astype(F32)


def call(body, args, specs, outs, scratch, ident=None):
    extra = {} if ident is None else {"collective_id": ident, "has_side_effects": True}
    return pl.pallas_call(
        body,
        out_shape=[jax.ShapeDtypeStruct(s, t) for s, t in outs],
        in_specs=specs,
        out_specs=[VM] * len(outs),
        scratch_shapes=scratch,
        compiler_params=pltpu.CompilerParams(vmem_limit_bytes=BIG, **extra),
    )(*args)


def on_device(features, cotangent, conv_one, down_weight, conv_two, patch_home, patch_links):
    n, dps = lax.axis_size("space"), lax.axis_size("dp")
    group = 8 if n % 8 == 0 else n
    chips = group // 2
    slots, c1 = features.shape[1], features.shape[2]
    c2 = conv_two.shape[0] * dps
    me = lax.axis_index("space")
    one, two = Level(PXY, PZ), Level(PXY // 2, PZ // 2)
    pack = Pack(conv_one.shape, down_weight.shape, conv_two.shape, group)

    own = patch_home[None, :] == (me * slots + jnp.arange(slots, dtype=jnp.int32))[:, None]
    live = jnp.any(own, axis=1).astype(F32)
    ids = jnp.arange(patch_home.shape[0], dtype=jnp.int32)
    codes = (me - 2) * slots + jnp.arange(5 * slots, dtype=jnp.int32)
    target = jnp.max(jnp.where(own[:, :, None], patch_links[None], -1), axis=1)
    source = jnp.max(jnp.where(target[:, :, None] == ids, patch_home, -1), axis=2)
    sel = ((source.T[:, :, None] == codes) & (source.T[:, :, None] >= 0)).astype(F32).reshape(-1)

    field = features[0]
    dma = pltpu.SemaphoreType.DMA
    rx, ry, full = call(
        functools.partial(start_kernel, n, dps, group, one, slots, pack),
        (field, sel, one.face_y(), one.rim_to_face_y(), conv_one, down_weight, conv_two),
        [VM, SM, VM, VM, VM, VM, VM],
        [((slots, c1, 128), BF), ((slots, c1, 256), BF), ((dps, pack.rows, pack.total), BF)],
        [pltpu.VMEM((pack.rows, pack.total), BF), pltpu.VMEM((dps, pack.rows, pack.total), BF),
         dma((dps - 1,)), dma((dps - 1,)), dma((dps - 1, chips - 1)), dma((dps - 1, chips - 1)),
         dma((dps - 1, chips)), dma((dps - 1, chips))]
        + halo_scratch(slots, c1),
        0,
    )

    cells_two = two.cells
    perm = []
    spot = []
    kind = np.full((1, one.out), -1, np.int32)
    for x, y, k in one.all():
        e = (x % 2) * 4 + (y % 2) * 2 + k % 2
        small = two.cell(x // 2, y // 2, k // 2)
        at = one.pos(x, y, k)
        perm.append((at, e * cells_two + small))
        spot.append((small, at))
        kind[0, at] = e
    padded, pre, split, reduced = call(
        functools.partial(first_kernel, one, slots, pack, dps),
        (field, rx, ry, one.place(), one.place_x(), one.place_y(), onehot(one.out, one.cells, perm), full),
        [VM] * 8,
        [((slots, c1, one.wide), BF), ((slots, c1, one.out), F32), ((slots, 8 * c1, cells_two), BF),
         ((slots, c2, cells_two), BF)],
        [pltpu.VMEM((c1, conv_one.shape[1]), BF), pltpu.VMEM((27 * c1, one.out), BF)],
    )

    sides = [(s, f) for s in range(slots) for f in range(2)]
    last = two.xy - 1
    place_of = {}
    for i, (s, f) in enumerate(sides):
        for k in range(two.z):
            for y in range(two.xy):
                place_of["x", s, f, y, k] = i * two.yz + y * two.z + k
            for xe in range(two.xy + 2):
                place_of["y", s, f, xe, k] = i * (two.xy + 2) * two.z + xe * two.z + k
    send_x, send_y, rim_y = [], [], []
    pad_x, pad_y, g_y, b_y, g_x, b_x = ([[] for s in range(slots)] for unused in range(6))
    for (axis, s, f, a, k), lane in place_of.items():
        inner = (0, last)[f]
        rim = (two.xy, -1)[f]
        far = (-1, two.xy)[f]
        near_cell = (last, 0)[f]
        if axis == "x":
            send_x.append((s * two.cells + two.cell(inner, a, k), lane))
            pad_x[s].append((lane, two.pad(rim, a, k)))
            g_x[s].append((two.pad(far, a, k), lane))
            b_x[s].append((lane, two.cell(near_cell, a, k)))
            for g in range(2):
                if a == (0, last)[g]:
                    rim_y.append((lane, place_of["y", s, g, rim + 1, k]))
        else:
            if 0 < a <= two.xy:
                send_y.append((s * two.cells + two.cell(a - 1, inner, k), lane))
            pad_y[s].append((lane, two.pad(a - 1, rim, k)))
            g_y[s].append((two.pad(a - 1, far, k), lane))
            b_y[s].append((lane, two.pad(a - 1, near_cell, k)))

    def stack(rows, cols, lists):
        return jnp.stack([onehot(rows, cols, pairs) for pairs in lists])

    def route(first, length):
        lane = np.arange(128)
        used = lane < 2 * slots * length
        same = (lane % length)[:, None] == (lane % length)[None, :]
        side = lane // length
        same &= (side % 2)[:, None] == (side % 2)[None, :]
        same &= used[:, None] & used[None, :]
        slot = jnp.asarray(np.where(used, side // 2, 0), jnp.int32)
        wanted = jnp.stack([source[:, first + 1], source[:, first]], axis=1)
        wanted = jnp.broadcast_to(wanted[:, :, None], (slots, 2, length)).reshape(-1)
        wanted = jnp.pad(wanted, (0, 128 - wanted.shape[0]), constant_values=-1)
        base = (me - 2 + jnp.arange(5, dtype=jnp.int32)) * slots
        hit = wanted[None, None, :] == base[:, None, None] + slot[None, :, None]
        hit = hit & jnp.asarray(same)[None] & (wanted >= 0)[None, None, :]
        return hit.astype(BF)

    way_x, way_y = route(0, two.yz), route(2, (two.xy + 2) * two.z)
    rx2, ry2 = call(
        functools.partial(halo_kernel, n, two, slots),
        (reduced, way_x, way_y, onehot(slots * cells_two, 128, send_x), onehot(slots * cells_two, 128, send_y),
         onehot(128, 128, rim_y)),
        [VM] * 6,
        [((c2, 128), BF), ((c2, 128), BF)],
        packed_scratch(c2),
        1,
    )

    scale = float(dps * patch_links.shape[0] * cells_two) ** (-0.5)
    trim = [(two.pos(*c), two.cell(*c)) for c in two.all()]
    level, dw_two, gp = call(
        functools.partial(second_kernel, two, slots, pack, dps, scale),
        (reduced, rx2, ry2, two.place(), stack(128, two.wide, pad_x), stack(128, two.wide, pad_y),
         onehot(two.out, cells_two, trim),
         onehot(cells_two, two.out, [(b, a) for a, b in trim]), cotangent[0], live, full),
        [VM] * 9 + [SM, VM],
        [((slots, c2, cells_two), BF), ((c2, 27 * c2), BF), ((slots, c2, two.out), F32)],
        [pltpu.VMEM((27 * c2, slots * two.out), BF), pltpu.VMEM((27 * c2, slots * two.out), BF),
         pltpu.VMEM((c2, 27 * c2), BF), pltpu.VMEM((3, c2, 256 + two.out), BF)],
    )

    dense = [(two.pad(*c), two.cell(*c)) for c in two.all()]
    [gr] = call(
        functools.partial(back_kernel, n, slots),
        (gp, way_x, way_y, stack(two.out, 128, g_y), stack(128, two.out, b_y), stack(two.out, 128, g_x),
         onehot(two.out, cells_two, dense), stack(128, cells_two, b_x)),
        [VM] * 8,
        [((slots, c2, cells_two), BF)],
        packed_scratch(c2),
        2,
    )

    dw_one, dw_down = call(
        functools.partial(last_kernel, one, slots, pack, dps),
        (gr, split, pre, padded, onehot(cells_two, one.out, spot), jnp.asarray(kind), full),
        [VM] * 7,
        [((c1, 27 * c1), BF), ((c2, 8 * c1), BF)],
        [pltpu.VMEM((27 * c1, one.out), BF)],
    )

    part = (dps, pack.rows, pack.part)
    [fin] = call(
        functools.partial(reduce_kernel, n, dps, group, pack),
        (dw_one, dw_down, dw_two),
        [VM] * 3,
        [((pack.rows, pack.total), BF)],
        [pltpu.VMEM((dps, pack.rows, pack.total), BF), pltpu.VMEM((chips,) + part, BF),
         pltpu.VMEM((chips - 1,) + part, BF), pltpu.VMEM((chips - 1,) + part, BF),
         pltpu.VMEM(part, BF), pltpu.VMEM((dps - 1, pack.rows, pack.part), BF),
         pltpu.VMEM((pack.rows, pack.total), BF)]
        + [dma((k,)) for k in (chips, chips, chips - 1, chips - 1, dps - 1, dps - 1, chips - 1, chips - 1, chips, chips)],
        3,
    )
    outs = call(
        functools.partial(unfold_kernel, pack),
        (fin,),
        [VM],
        [(conv_one.shape, F32), (down_weight.shape, F32), (conv_two.shape, F32)],
        [],
    )
    if n > group:
        rings = [[a + m for a in range(0, n, group)] for m in range(group)]
        outs = [lax.psum(o, "space", axis_index_groups=rings) for o in outs]
    return (level[None], outs[0], outs[1], outs[2])


def solution(mesh):
    weights = P("dp", None)
    slabs = P("dp", "space", None, None)
    return jax.shard_map(
        on_device,
        mesh=mesh,
        in_specs=(slabs, slabs, weights, weights, weights, P(), P()),
        out_specs=(slabs, weights, weights, weights),
        check_vma=False,
    )
```

```python
import functools

import jax
import jax.numpy as jnp
import numpy as np
from jax import lax
from jax.experimental import pallas as pl
from jax.experimental.pallas import tpu as pltpu
from jax.sharding import PartitionSpec as P

PXY = 16
PZ = 4
LEAD = 8
BF = jnp.bfloat16
F32 = jnp.float32
MESH = pl.DeviceIdType.MESH
VM = pl.BlockSpec(memory_space=pltpu.VMEM)
SM = pl.BlockSpec(memory_space=pltpu.SMEM)
BIG = 58 * 1024 * 1024


def up128(value):
    return -(-value // 128) * 128


def dot(a, b):
    return jnp.dot(a, b, preferred_element_type=F32)


def dot_nt(a, b):
    return lax.dot_general(a, b, (((1,), (1,)), ((), ())), preferred_element_type=F32)


def sigmoid(v):
    return 1.0 / (1.0 + jnp.exp(-v))


def onehot(rows, cols, pairs):
    m = np.zeros((rows, cols), np.float32)
    for r, c in pairs:
        m[r, c] = 1.0
    return jnp.asarray(m, BF)


class Level:
    def __init__(self, xy, z):
        self.xy, self.z = xy, z
        self.yz = xy * z
        self.cells = xy * xy * z
        self.stride = (xy + 2) * z
        self.out = up128(xy * self.stride)
        self.wide = up128(LEAD + self.out + 2 * self.stride + z + 1)

    def cell(self, x, y, k):
        return x * self.yz + y * self.z + k

    def pad(self, x, y, k):
        return LEAD + (x + 1) * self.stride + (y + 1) * self.z + k

    def pos(self, x, y, k):
        return x * self.stride + (y + 1) * self.z + k

    def shift(self, tap):
        dx, dy, dz = tap // 9 - 1, (tap // 3) % 3 - 1, tap % 3 - 1
        return LEAD + self.stride * (1 + dx) + self.z * dy + dz

    def all(self):
        r, q = range(self.xy), range(self.z)
        return [(x, y, k) for x in r for y in r for k in q]

    def face_y(self):
        last = self.xy - 1
        r, q = range(self.xy), range(self.z)
        pairs = []
        for x in r:
            for k in q:
                pairs.append((self.cell(x, 0, k), (x + 1) * self.z + k))
                pairs.append((self.cell(x, last, k), 128 + (x + 1) * self.z + k))
        return onehot(self.cells, 256, pairs)

    def rim_to_face_y(self):
        last = self.xy - 1
        pairs = []
        for k in range(self.z):
            for base, xe in ((0, self.xy + 1), (64, 0)):
                pairs.append((base + k, xe * self.z + k))
                pairs.append((base + last * self.z + k, 128 + xe * self.z + k))
        return onehot(128, 256, pairs)

    def place_x(self):
        pairs = []
        for y in range(self.xy):
            for k in range(self.z):
                pairs.append((y * self.z + k, self.pad(self.xy, y, k)))
                pairs.append((64 + y * self.z + k, self.pad(-1, y, k)))
        return onehot(128, self.wide, pairs)

    def place_y(self):
        pairs = []
        for xe in range(self.xy + 2):
            for k in range(self.z):
                pairs.append((xe * self.z + k, self.pad(xe - 1, self.xy, k)))
                pairs.append((128 + xe * self.z + k, self.pad(xe - 1, -1, k)))
        return onehot(256, self.wide, pairs)

    def place(self):
        return onehot(self.cells, self.wide, [(self.cell(*c), self.pad(*c)) for c in self.all()])


def barrier(lists):
    sem = pltpu.get_barrier_semaphore()
    for target in lists:
        pl.semaphore_signal(sem, inc=1, device_id=target, device_id_type=MESH)
    pl.semaphore_wait(sem, len(lists))


def near(n):
    me = lax.axis_index("space")
    return {k: lax.rem(me + k + n, n) for k in (-2, -1, 1, 2)}


def members(n, group):
    me = lax.axis_index("space")
    inside = lax.rem(me, group)
    base = me - inside
    core, chip = lax.rem(inside, 2), inside // 2
    chips = group // 2
    others = [lax.rem(chip + k, chips) for k in range(1, chips)]
    return core, chip, base + 2 * chip + 1 - core, others, [base + 2 * t + core for t in others]


def swap(n, src, dst, reach, send, recv):
    ids = near(n)
    order = [k for k in range(-reach, reach + 1) if k != 0]
    copies = []
    for i, k in enumerate(order):
        copies.append(
            pltpu.make_async_remote_copy(
                src_ref=src,
                dst_ref=dst.at[i],
                send_sem=send.at[i],
                recv_sem=recv.at[i],
                device_id={"space": ids[-k]},
                device_id_type=MESH,
            )
        )
    for c in copies:
        c.start()
    return order, copies


def select(sel_ref, slots, own, got, order, upper, lower):
    width = own.shape[2]
    first = lax.broadcasted_iota(jnp.int32, (1, width), 1) < width // 2
    blocks = [(k, s, (own[s] if k == 0 else got[order.index(k), s]).astype(F32))
              for k in [0] + order for s in range(slots)]
    result = []
    for t in range(slots):
        total = None
        for k, s, block in blocks:
            at = lambda side: sel_ref[((side * slots + t) * 5 + k + 2) * slots + s]
            term = block * jnp.where(first, at(upper), at(lower))
            total = term if total is None else total + term
        result.append(total.astype(BF))
    return result


def halo_body(n, lv, slots, field, sel, e_face, e_rim, rx, ry, sx, sy, gx, gy, xs, xr, ys, yr, early, between):
    chan = field.shape[1]
    last = lv.cells - lv.yz
    sx[...] = jnp.zeros_like(sx)
    sx[:, :, 0 : lv.yz] = field[:, :, 0 : lv.yz]
    sx[:, :, 64 : 64 + lv.yz] = field[:, :, last : lv.cells]
    order, copies = swap(n, sx, gx, 1, xs, xr)
    early()
    base = dot(field[...].reshape(slots * chan, lv.cells), e_face[...])
    for c in copies:
        c.wait()
    rims = select(sel, slots, sx, gx, order, 1, 0)
    for s in range(slots):
        rx[s] = rims[s]
        sy[s] = (base[s * chan : (s + 1) * chan] + dot(rims[s], e_rim[...])).astype(BF)
    order, copies = swap(n, sy, gy, 2, ys, yr)
    between()
    for c in copies:
        c.wait()
    rims = select(sel, slots, sy, gy, order, 3, 2)
    for s in range(slots):
        ry[s] = rims[s]


def halo_scratch(slots, chan):
    return [
        pltpu.VMEM((slots, chan, 128), BF),
        pltpu.VMEM((slots, chan, 256), BF),
        pltpu.VMEM((2, slots, chan, 128), BF),
        pltpu.VMEM((4, slots, chan, 256), BF),
        pltpu.SemaphoreType.DMA((2,)),
        pltpu.SemaphoreType.DMA((2,)),
        pltpu.SemaphoreType.DMA((4,)),
        pltpu.SemaphoreType.DMA((4,)),
    ]


class Pack:
    def __init__(self, one, down, two, group):
        self.one, self.down, self.two = one, down, two
        self.rows = two[0]
        self.half = up128(-(-one[1] // 2))
        self.at_down = two[1]
        self.at_one = two[1] + down[1]
        self.total = -(-(self.at_one + self.half) // (group * 128)) * group * 128
        self.part = self.total // group
        self.rest = one[1] - self.half

    def put(self, dst, one, down, two):
        low = self.one[0]
        a = self.at_one
        dst[:, 0 : self.at_down] = two
        dst[:, self.at_down : a] = down
        dst[:, a:] = jnp.zeros((self.rows, self.total - a), dst.dtype)
        dst[0:low, a : a + self.half] = one[:, 0 : self.half]
        dst[low : 2 * low, a : a + self.rest] = one[:, self.half :]

    def lanes(self, index):
        return pl.ds(pl.multiple_of(index * self.part, 128), self.part)


def remote(src, dst, send, recv, target):
    return pltpu.make_async_remote_copy(
        src_ref=src, dst_ref=dst, send_sem=send, recv_sem=recv, device_id=target, device_id_type=MESH
    )


def start_kernel(n, dps, group, lv, slots, pack, field, sel, e_face, e_rim, one, down, two, rx, ry, full,
                 packed, gath, zs, zr, ms, mr, ps, pr, *halo):
    dp = lax.axis_index("dp")
    core, chip, sibling, others, targets = members(n, group)
    chips = group // 2
    peers = [lax.rem(dp + k, dps) for k in range(1, dps)]
    pack.put(packed, one[...], down[...], two[...])
    barrier([{"space": t} for t in near(n).values()] + [{"space": t} for t in targets + [sibling]]
            + [{"dp": t} for t in peers])
    lanes = pack.lanes(core * chips + chip)
    zc, mc, sc = [], [], []
    for i, t in enumerate(peers):
        zc.append(remote(packed.at[:, lanes], gath.at[dp, :, lanes], zs.at[i], zr.at[i], {"dp": t}))
    shares = [lax.rem(dp + dps - 1 - i, dps) for i in range(dps - 1)]

    def early():
        for c in zc:
            c.start()
        gath[dp] = packed[...]

    def between():
        for i in range(dps - 1):
            zc[i].wait()
            block = gath.at[shares[i], :, lanes]
            for j, t in enumerate(targets):
                c = remote(block, block, ms.at[i, j], mr.at[i, j], {"space": t})
                c.start()
                mc.append(c)
            c = remote(block, block, ps.at[i, chips - 1], pr.at[i, chips - 1], {"space": sibling})
            c.start()
            sc.append(c)

    halo_body(n, lv, slots, field, sel, e_face, e_rim, rx, ry, *halo, early, between)
    for i in range(dps - 1):
        for j in range(chips - 1):
            mc[i * (chips - 1) + j].wait()
            sender = lax.rem(chip + chips - 1 - j, chips)
            block = gath.at[shares[i], :, pack.lanes(core * chips + sender)]
            c = remote(block, block, ps.at[i, j], pr.at[i, j], {"space": sibling})
            c.start()
            sc.append(c)
    for c in sc:
        c.wait()
    full[...] = gath[...]


def routed(block, got, order, route):
    total = dot(block[...], route[2])
    for i, k in enumerate(order):
        total = total + dot(got[i], route[k + 2])
    return total.astype(BF)


def halo_kernel(n, lv, slots, field, way_x, way_y, e_x, e_y, e_rim, rx, ry, sx, sy, gx, gy, xs, xr, ys, yr):
    wide = jnp.concatenate([field[s] for s in range(slots)], axis=1)
    sx[...] = dot(wide, e_x[...]).astype(BF)
    barrier([{"space": t} for t in near(n).values()])
    order, copies = swap(n, sx, gx, 1, xs, xr)
    base = dot(wide, e_y[...])
    for c in copies:
        c.wait()
    rim = routed(sx, gx, order, way_x)
    rx[...] = rim
    sy[...] = (base + dot(rim, e_rim[...])).astype(BF)
    order, copies = swap(n, sy, gy, 2, ys, yr)
    for c in copies:
        c.wait()
    ry[...] = routed(sy, gy, order, way_y)


def packed_scratch(chan):
    return [
        pltpu.VMEM((chan, 128), BF),
        pltpu.VMEM((chan, 128), BF),
        pltpu.VMEM((2, chan, 128), BF),
        pltpu.VMEM((4, chan, 128), BF),
        pltpu.SemaphoreType.DMA((2,)),
        pltpu.SemaphoreType.DMA((2,)),
        pltpu.SemaphoreType.DMA((4,)),
        pltpu.SemaphoreType.DMA((4,)),
    ]


def columns(lv, padded, chan, store):
    lane = lax.broadcasted_iota(jnp.int32, padded.shape, 1) % lv.z
    zero = jnp.zeros_like(padded)
    kinds = [jnp.where(lane == lv.z - 1, zero, padded), padded, jnp.where(lane == 0, zero, padded)]
    for tap in range(27):
        a = lv.shift(tap)
        store(tap, kinds[tap % 3][:, a : a + lv.out])


def unfold_one(pack, dps, full, w1):
    low = pack.one[0]
    a = pack.at_one
    for d in range(dps):
        w1[d * low : (d + 1) * low, 0 : pack.half] = full[d, 0:low, a : a + pack.half]
        w1[d * low : (d + 1) * low, pack.half :] = full[d, low : 2 * low, a : a + pack.rest]


def first_kernel(lv, slots, pack, dps, field, rx, ry, e_place, e_x, e_y, e_perm, full,
                 padded, pre, split, reduced, w1, xcol):
    chan = field.shape[1]
    unfold_one(pack, dps, full, w1)
    rows = slots * chan
    pad = (dot(field[...].reshape(rows, lv.cells), e_place[...])
           + dot(rx[...].reshape(rows, 128), e_x[...])
           + dot(ry[...].reshape(rows, 256), e_y[...])).astype(BF)
    down = full[:, :, pack.at_down : pack.at_one].reshape(dps * pack.rows, pack.down[1])
    cells = lv.cells // 8
    for s in range(slots):
        mine = pad[s * chan : (s + 1) * chan]
        padded[s] = mine

        def store(tap, value):
            xcol[tap * chan : (tap + 1) * chan] = value

        columns(lv, mine, chan, store)
        value = dot(w1[...], xcol[...])
        pre[s] = value
        hidden = (value * sigmoid(value)).astype(BF)
        parts = dot(hidden, e_perm[...]).astype(BF)
        stacked = jnp.concatenate([parts[:, e * cells : (e + 1) * cells] for e in range(8)], axis=0)
        split[s] = stacked
        reduced[s] = dot(down, stacked).astype(BF)


def second_kernel(lv, slots, pack, dps, scale, field, rx, ry, e_place, e_x, e_y, e_trim, e_spread, cot, live, full,
                  level, dw, gp, xcol, gcol, wt, gbuf):
    chan = field.shape[1]
    w2 = full[:, :, 0 : pack.at_down].reshape(dps * pack.rows, pack.at_down)
    out = lv.out
    for s in range(slots):
        def store(tap, value):
            xcol[tap * chan : (tap + 1) * chan, s * out : (s + 1) * out] = value

        pad = dot(field[s], e_place[...]) + dot(rx[...], e_x[s]) + dot(ry[...], e_y[s])
        columns(lv, pad.astype(BF), chan, store)
    pre = dot(w2, xcol[...])
    gbuf[...] = jnp.zeros_like(gbuf)
    lane = lax.broadcasted_iota(jnp.int32, (1, out), 1) % lv.z
    grads = []
    for s in range(slots):
        v = pre[:, s * out : (s + 1) * out]
        sg = sigmoid(v)
        act = dot((v * sg).astype(BF), e_trim[...])
        alive = live[s] > 0.5
        level[s] = jnp.where(alive, act, 0.0).astype(BF)
        inc = dot(cot[s], e_spread[...])
        g = jnp.where(alive, inc * (sg * (1.0 + v * (1.0 - sg))) * scale, 0.0)
        grads.append(g.astype(BF))
        for d in range(3):
            keep = lane >= 0 if d == 1 else (lane != 0 if d == 0 else lane != lv.z - 1)
            gbuf[d, :, 128 : 128 + out] = jnp.where(keep, g, 0.0).astype(BF)
        for tap in range(27):
            a = 128 - lv.shift(tap)
            gcol[tap * chan : (tap + 1) * chan, s * out : (s + 1) * out] = gbuf[tap % 3, :, a : a + out]
    for tap in range(27):
        wt[:, tap * chan : (tap + 1) * chan] = w2[:, tap * chan : (tap + 1) * chan].astype(F32).T.astype(BF)
    back = dot(wt[...], gcol[...])
    for s in range(slots):
        gp[s] = back[:, s * out : (s + 1) * out]
    dw[...] = dot_nt(jnp.concatenate(grads, axis=1), xcol[...]).astype(BF)


def back_kernel(n, slots, gp, way_x, way_y, e_gy, e_by, e_gx, e_dense, e_bx, out,
                sx, sy, gx, gy, xs, xr, ys, yr):
    total = None
    for s in range(slots):
        part = dot(gp[s].astype(BF), e_gy[s])
        total = part if total is None else total + part
    sy[...] = total.astype(BF)
    barrier([{"space": t} for t in near(n).values()])
    order, copies = swap(n, sy, gy, 2, ys, yr)
    for c in copies:
        c.wait()
    back = routed(sy, gy, order, way_y)
    dense = []
    total = None
    for s in range(slots):
        w = gp[s] + dot(back, e_by[s])
        hi = w.astype(BF)
        low = (w - hi.astype(F32)).astype(BF)
        part = dot(hi, e_gx[s])
        total = part if total is None else total + part
        dense.append((hi, low))
    sx[...] = total.astype(BF)
    order, copies = swap(n, sx, gx, 1, xs, xr)
    dense = [dot(hi, e_dense[...]) + dot(low, e_dense[...]) for hi, low in dense]
    for c in copies:
        c.wait()
    back = routed(sx, gx, order, way_x)
    for s in range(slots):
        out[s] = (dense[s] + dot(back, e_bx[s])).astype(BF)


def last_kernel(lv, slots, pack, dps, gr, split, pre, padded, e_up, kind, full, dw_one, dw_down, xcol):
    chan = pre.shape[1]
    down = full[:, :, pack.at_down : pack.at_one].reshape(dps * pack.rows, pack.down[1])
    down_t = down.astype(F32).T.astype(BF)
    total_down = None
    total_one = None
    for s in range(slots):
        g = gr[s]
        part = dot_nt(g, split[s])
        total_down = part if total_down is None else total_down + part
        up = dot(g, e_up[...]).astype(BF)
        eight = dot(down_t, up)
        gh = None
        for e in range(8):
            term = jnp.where(kind[...] == e, eight[e * chan : (e + 1) * chan], 0.0)
            gh = term if gh is None else gh + term
        v = pre[s]
        sg = sigmoid(v)
        g1 = (gh * (sg * (1.0 + v * (1.0 - sg)))).astype(BF)

        def store(tap, value):
            xcol[tap * chan : (tap + 1) * chan] = value

        columns(lv, padded[s], chan, store)
        part = dot_nt(g1, xcol[...])
        total_one = part if total_one is None else total_one + part
    dw_down[...] = total_down.astype(BF)
    dw_one[...] = total_one.astype(BF)


def reduce_kernel(n, dps, group, pack, one, down, two, out,
                  packed, r0, a1, rs, acc, zb, fin, ps, pr, ms, mr, zs, zr, fs, fr, qs, qr):
    dp = lax.axis_index("dp")
    core, chip, sibling, others, targets = members(n, group)
    chips = group // 2
    peers = [lax.rem(dp + k, dps) for k in range(1, dps)]
    r1, r2 = pack.one[0], pack.rows
    for d in range(dps):
        pack.put(packed.at[d], one[d * r1 : (d + 1) * r1], down[d * r2 : (d + 1) * r2], two[d * r2 : (d + 1) * r2])
    barrier([{"space": t} for t in targets + [sibling]] + [{"dp": t} for t in peers])
    order = others + [chip]
    copies = []
    for j, t in enumerate(order):
        c = remote(packed.at[:, :, pack.lanes((1 - core) * chips + t)], r0.at[j], ps.at[j], pr.at[j],
                   {"space": sibling})
        c.start()
        copies.append(c)
    sent = []
    for j, t in enumerate(order):
        copies[j].wait()
        value = packed[:, :, pack.lanes(core * chips + t)].astype(F32) + r0[j].astype(F32)
        if j < chips - 1:
            a1[j] = value.astype(BF)
            c = remote(a1.at[j], rs.at[j], ms.at[j], mr.at[j], {"space": targets[j]})
            c.start()
            sent.append(c)
    for j, c in enumerate(sent):
        c.wait()
        value = value + rs[j].astype(F32)
    acc[...] = value.astype(BF)
    copies = []
    for j, t in enumerate(peers):
        c = remote(acc.at[t], zb.at[j], zs.at[j], zr.at[j], {"dp": t})
        c.start()
        copies.append(c)
    total = acc[dp].astype(F32)
    for j, c in enumerate(copies):
        c.wait()
        total = total + zb[j].astype(F32)
    lanes = pack.lanes(core * chips + chip)
    fin[:, lanes] = total.astype(BF)
    block = fin.at[:, lanes]
    copies, last = [], []
    for j, t in enumerate(targets):
        c = remote(block, block, fs.at[j], fr.at[j], {"space": t})
        c.start()
        copies.append(c)
    c = remote(block, block, qs.at[chips - 1], qr.at[chips - 1], {"space": sibling})
    c.start()
    last.append(c)
    for j, c in enumerate(copies):
        c.wait()
        block = fin.at[:, pack.lanes(core * chips + lax.rem(chip + chips - 1 - j, chips))]
        c = remote(block, block, qs.at[j], qr.at[j], {"space": sibling})
        c.start()
        last.append(c)
    for c in last:
        c.wait()
    out[...] = fin[...]


def unfold_kernel(pack, fin, o_one, o_down, o_two):
    r1 = pack.one[0]
    a = pack.at_one
    o_two[...] = fin[:, 0 : pack.at_down].astype(F32)
    o_down[...] = fin[:, pack.at_down : a].astype(F32)
    o_one[:, 0 : pack.half] = fin[0:r1, a : a + pack.half].astype(F32)
    o_one[:, pack.half :] = fin[r1 : 2 * r1, a : a + pack.rest].astype(F32)


def table_kernel(slots, home, links, same_x, same_y, sel, live, way_x, way_y, src):
    me = lax.axis_index("space")
    for s in range(slots):
        live[s] = jnp.float32(0.0)
        for f in range(4):
            src[s * 4 + f] = jnp.int32(-1)

    @pl.loop(0, home.shape[0])
    def _(p):
        slot = home[p] - me * slots

        @pl.when((slot >= 0) & (slot < slots))
        def _():
            live[slot] = jnp.float32(1.0)
            for f in range(4):
                q = links[p * 4 + f]
                src[slot * 4 + f] = jnp.where(q >= 0, home[jnp.maximum(q, 0)], -1)

    for f in range(4):
        for s in range(slots):
            code = src[s * 4 + f]
            for k in range(5):
                for t in range(slots):
                    hit = (code >= 0) & (code == (me + k - 2) * slots + t)
                    sel[((f * slots + s) * 5 + k) * slots + t] = jnp.where(hit, jnp.float32(1.0), jnp.float32(0.0))
    for way, same, first in ((way_x, same_x, 0), (way_y, same_y, 2)):
        width = same.shape[2]
        group = same[1]
        wanted = jnp.full((width, width), -1, jnp.int32)
        for s in range(slots):
            for f in range(2):
                wanted = jnp.where(group == 2 * s + f, src[s * 4 + first + 1 - f], wanted)
        slot = same[0]
        meets = (slot >= 0) & (wanted >= 0)
        for k in range(5):
            hit = meets & (wanted == slot + (me + k - 2) * slots)
            way[k] = jnp.where(hit, 1.0, 0.0).astype(BF)


def call(body, args, specs, outs, scratch, ident=None):
    extra = {} if ident is None else {"collective_id": ident, "has_side_effects": True}
    return pl.pallas_call(
        body,
        out_shape=[jax.ShapeDtypeStruct(s, t) for s, t in outs],
        in_specs=specs,
        out_specs=[VM] * len(outs),
        scratch_shapes=scratch,
        compiler_params=pltpu.CompilerParams(vmem_limit_bytes=BIG, **extra),
    )(*args)


def on_device(features, cotangent, conv_one, down_weight, conv_two, patch_home, patch_links):
    n, dps = lax.axis_size("space"), lax.axis_size("dp")
    group = 8 if n % 8 == 0 else n
    chips = group // 2
    slots, c1 = features.shape[1], features.shape[2]
    c2 = conv_two.shape[0] * dps
    one, two = Level(PXY, PZ), Level(PXY // 2, PZ // 2)
    pack = Pack(conv_one.shape, down_weight.shape, conv_two.shape, group)

    def meeting(length):
        lane = np.arange(128)
        used = lane < 2 * slots * length
        same = (lane % length)[:, None] == (lane % length)[None, :]
        side = lane // length
        same &= (side % 2)[:, None] == (side % 2)[None, :]
        same &= used[:, None] & used[None, :]
        slot = np.where(same, (side // 2)[:, None], -1)
        group_of = np.where(same, side[None, :], -1)
        return jnp.asarray(np.stack([slot, group_of]), jnp.int32)

    sel, live, way_x, way_y = pl.pallas_call(
        functools.partial(table_kernel, slots),
        out_shape=[jax.ShapeDtypeStruct((20 * slots * slots,), F32), jax.ShapeDtypeStruct((slots,), F32),
                   jax.ShapeDtypeStruct((5, 128, 128), BF), jax.ShapeDtypeStruct((5, 128, 128), BF)],
        in_specs=[SM, SM, VM, VM],
        out_specs=[SM, SM, VM, VM],
        scratch_shapes=[pltpu.SMEM((4 * slots,), jnp.int32)],
    )(patch_home, patch_links.reshape(-1), meeting(two.yz), meeting((two.xy + 2) * two.z))

    field = features[0]
    dma = pltpu.SemaphoreType.DMA
    rx, ry, full = call(
        functools.partial(start_kernel, n, dps, group, one, slots, pack),
        (field, sel, one.face_y(), one.rim_to_face_y(), conv_one, down_weight, conv_two),
        [VM, SM, VM, VM, VM, VM, VM],
        [((slots, c1, 128), BF), ((slots, c1, 256), BF), ((dps, pack.rows, pack.total), BF)],
        [pltpu.VMEM((pack.rows, pack.total), BF), pltpu.VMEM((dps, pack.rows, pack.total), BF),
         dma((dps - 1,)), dma((dps - 1,)), dma((dps - 1, chips - 1)), dma((dps - 1, chips - 1)),
         dma((dps - 1, chips)), dma((dps - 1, chips))]
        + halo_scratch(slots, c1),
        0,
    )

    cells_two = two.cells
    perm = []
    spot = []
    kind = np.full((1, one.out), -1, np.int32)
    for x, y, k in one.all():
        e = (x % 2) * 4 + (y % 2) * 2 + k % 2
        small = two.cell(x // 2, y // 2, k // 2)
        at = one.pos(x, y, k)
        perm.append((at, e * cells_two + small))
        spot.append((small, at))
        kind[0, at] = e
    padded, pre, split, reduced = call(
        functools.partial(first_kernel, one, slots, pack, dps),
        (field, rx, ry, one.place(), one.place_x(), one.place_y(), onehot(one.out, one.cells, perm), full),
        [VM] * 8,
        [((slots, c1, one.wide), BF), ((slots, c1, one.out), F32), ((slots, 8 * c1, cells_two), BF),
         ((slots, c2, cells_two), BF)],
        [pltpu.VMEM((c1, conv_one.shape[1]), BF), pltpu.VMEM((27 * c1, one.out), BF)],
    )

    sides = [(s, f) for s in range(slots) for f in range(2)]
    last = two.xy - 1
    place_of = {}
    for i, (s, f) in enumerate(sides):
        for k in range(two.z):
            for y in range(two.xy):
                place_of["x", s, f, y, k] = i * two.yz + y * two.z + k
            for xe in range(two.xy + 2):
                place_of["y", s, f, xe, k] = i * (two.xy + 2) * two.z + xe * two.z + k
    send_x, send_y, rim_y = [], [], []
    pad_x, pad_y, g_y, b_y, g_x, b_x = ([[] for s in range(slots)] for unused in range(6))
    for (axis, s, f, a, k), lane in place_of.items():
        inner = (0, last)[f]
        rim = (two.xy, -1)[f]
        far = (-1, two.xy)[f]
        near_cell = (last, 0)[f]
        if axis == "x":
            send_x.append((s * two.cells + two.cell(inner, a, k), lane))
            pad_x[s].append((lane, two.pad(rim, a, k)))
            g_x[s].append((two.pad(far, a, k), lane))
            b_x[s].append((lane, two.cell(near_cell, a, k)))
            for g in range(2):
                if a == (0, last)[g]:
                    rim_y.append((lane, place_of["y", s, g, rim + 1, k]))
        else:
            if 0 < a <= two.xy:
                send_y.append((s * two.cells + two.cell(a - 1, inner, k), lane))
            pad_y[s].append((lane, two.pad(a - 1, rim, k)))
            g_y[s].append((two.pad(a - 1, far, k), lane))
            b_y[s].append((lane, two.pad(a - 1, near_cell, k)))

    def stack(rows, cols, lists):
        return jnp.stack([onehot(rows, cols, pairs) for pairs in lists])

    rx2, ry2 = call(
        functools.partial(halo_kernel, n, two, slots),
        (reduced, way_x, way_y, onehot(slots * cells_two, 128, send_x), onehot(slots * cells_two, 128, send_y),
         onehot(128, 128, rim_y)),
        [VM] * 6,
        [((c2, 128), BF), ((c2, 128), BF)],
        packed_scratch(c2),
        1,
    )

    scale = float(dps * patch_links.shape[0] * cells_two) ** (-0.5)
    trim = [(two.pos(*c), two.cell(*c)) for c in two.all()]
    level, dw_two, gp = call(
        functools.partial(second_kernel, two, slots, pack, dps, scale),
        (reduced, rx2, ry2, two.place(), stack(128, two.wide, pad_x), stack(128, two.wide, pad_y),
         onehot(two.out, cells_two, trim),
         onehot(cells_two, two.out, [(b, a) for a, b in trim]), cotangent[0], live, full),
        [VM] * 9 + [SM, VM],
        [((slots, c2, cells_two), BF), ((c2, 27 * c2), BF), ((slots, c2, two.out), F32)],
        [pltpu.VMEM((27 * c2, slots * two.out), BF), pltpu.VMEM((27 * c2, slots * two.out), BF),
         pltpu.VMEM((c2, 27 * c2), BF), pltpu.VMEM((3, c2, 256 + two.out), BF)],
    )

    dense = [(two.pad(*c), two.cell(*c)) for c in two.all()]
    [gr] = call(
        functools.partial(back_kernel, n, slots),
        (gp, way_x, way_y, stack(two.out, 128, g_y), stack(128, two.out, b_y), stack(two.out, 128, g_x),
         onehot(two.out, cells_two, dense), stack(128, cells_two, b_x)),
        [VM] * 8,
        [((slots, c2, cells_two), BF)],
        packed_scratch(c2),
        2,
    )

    dw_one, dw_down = call(
        functools.partial(last_kernel, one, slots, pack, dps),
        (gr, split, pre, padded, onehot(cells_two, one.out, spot), jnp.asarray(kind), full),
        [VM] * 7,
        [((c1, 27 * c1), BF), ((c2, 8 * c1), BF)],
        [pltpu.VMEM((27 * c1, one.out), BF)],
    )

    part = (dps, pack.rows, pack.part)
    [fin] = call(
        functools.partial(reduce_kernel, n, dps, group, pack),
        (dw_one, dw_down, dw_two),
        [VM] * 3,
        [((pack.rows, pack.total), BF)],
        [pltpu.VMEM((dps, pack.rows, pack.total), BF), pltpu.VMEM((chips,) + part, BF),
         pltpu.VMEM((chips - 1,) + part, BF), pltpu.VMEM((chips - 1,) + part, BF),
         pltpu.VMEM(part, BF), pltpu.VMEM((dps - 1, pack.rows, pack.part), BF),
         pltpu.VMEM((pack.rows, pack.total), BF)]
        + [dma((k,)) for k in (chips, chips, chips - 1, chips - 1, dps - 1, dps - 1, chips - 1, chips - 1, chips, chips)],
        3,
    )
    outs = call(
        functools.partial(unfold_kernel, pack),
        (fin,),
        [VM],
        [(conv_one.shape, F32), (down_weight.shape, F32), (conv_two.shape, F32)],
        [],
    )
    if n > group:
        rings = [[a + m for a in range(0, n, group)] for m in range(group)]
        outs = [lax.psum(o, "space", axis_index_groups=rings) for o in outs]
    return (level[None], outs[0], outs[1], outs[2])


def solution(mesh):
    weights = P("dp", None)
    slabs = P("dp", "space", None, None)
    return jax.shard_map(
        on_device,
        mesh=mesh,
        in_specs=(slabs, slabs, weights, weights, weights, P(), P()),
        out_specs=(slabs, weights, weights, weights),
        check_vma=False,
    )
```
